32 devices in a mesh: groups: 2 (over y), tx: 4 (over z), ty: 2 (over x), tz: 2 (over core).
Axes of the slice: x: 2, y: 2, z: 4, core: 2. Of those that a mesh axis runs over, the one named last changes fastest.
Arguments:
- phase: float32 [8, 64, 128, 256], P(None, ('groups', 'tx'), 'ty', 'tz'), parts along dimension 1, may hold values from 0 to 0.25
- slot_grain: int32 [8, 2, 2, 8], P(('groups', 'tx'), 'ty', 'tz'), parts along dimension 0, may hold values from 0 to 63, as said below
- crowding: int32 [8, 2, 2], P(('groups', 'tx'), 'ty', 'tz'), parts along dimension 0, may hold values from 4 to 8, as said below
- grain_home: int32 [128], P('groups'), parts along dimension 0, may hold values from 0 to 63, each once
- grain_weight: float32 [128], P('groups'), parts along dimension 0, may hold values from 0.5 to 2
- grain_target: float32 [128], P('groups'), parts along dimension 0, may hold values from 0.5 to 4
Outputs:
- phase_out: float32 [8, 64, 128, 256], P(None, ('groups', 'tx'), 'ty', 'tz'), parts along dimension 1
The draws below stay inside these ranges and needn't reach their ends.
There are 2 independent parts, one for each index of `groups`. The reference program is written for one: setup_inputs(seed, part) draws one part's arguments, and reference() takes and returns one part's arrays. A program takes and returns all parts, laid end to end along the dimension named above; each array names one. Nothing has to cross between parts.
Inputs may be any that keep to these rules, and one draw needn't show every extreme that they name: `slot_grain`: within one tile the slots name distinct grains; tiles that share a face share grains. `crowding`: some tile has 8 live slots and some has 4.
All inputs are finite; a program needn't handle non-finite values.
Results may differ from the reference program's by a relative error of at most 0.0001.
Values sent between devices are 32-bit elements; how exact they have to be, the bound alone decides.
A program may use at most 64 MiB of HBM per device.

```python
import math
import jax
import jax.numpy as jnp
from jax import lax

SLOTS = 8
CX = 8
CY = 64
CZ = 128
STEPS = 2
TILES_X = 4
TILES_Y = 2
TILES_Z = 2
GRAINS = 64
NX = 32
NY = 128
NZ = 256


def draw_slot_grain(key, part):
    key = jax.random.fold_in(key, 11)
    first, second, third, fourth = jax.random.split(key, 4)
    regions = (TILES_X + 1) * (TILES_Y + 1) * (TILES_Z + 1)
    tiles = TILES_X * TILES_Y * TILES_Z
    rest = jax.random.permutation(first, GRAINS - 2) + 1
    shuffled = jnp.concatenate([jnp.array([GRAINS - 1, 0], jnp.int32), rest.astype(jnp.int32)])
    tile_x = jnp.arange(TILES_X)[:, None, None, None]
    tile_y = jnp.arange(TILES_Y)[None, :, None, None]
    tile_z = jnp.arange(TILES_Z)[None, None, :, None]
    corner = jnp.arange(SLOTS)[None, None, None, :]
    region = ((tile_x + corner // 4) * (TILES_Y + 1) + (tile_y + corner // 2 % 2)) * (TILES_Z + 1) + tile_z + corner % 2
    shared_ids = shuffled[region]
    tile_number = (tile_x * TILES_Y + tile_y) * TILES_Z + tile_z
    fresh_ids = shuffled[regions + tile_number]
    picked = jax.random.randint(second, (TILES_X, TILES_Y, TILES_Z, 1), 0, SLOTS)
    altered = (jax.random.randint(third, (TILES_X, TILES_Y, TILES_Z, 1), 0, 2) == 1) & (tile_number > 0)
    chosen = jnp.where(altered & (corner == picked), fresh_ids, shared_ids)
    orders = jax.vmap(lambda part_key: jax.random.permutation(part_key, SLOTS))(jax.random.split(fourth, tiles))
    orders = orders.reshape(TILES_X, TILES_Y, TILES_Z, SLOTS)
    return jnp.take_along_axis(chosen, orders, axis=3).astype(jnp.int32)


def draw_crowding(key, part):
    key = jax.random.fold_in(key, 23)
    first, second = jax.random.split(key)
    count = TILES_X * TILES_Y * TILES_Z
    values = jax.random.randint(first, (count,), 4, SLOTS + 1)
    where_full = jax.random.randint(second, (), 0, count)
    values = values.at[where_full].set(SLOTS)
    values = values.at[(where_full + 1) % count].set(4)
    return values.reshape(TILES_X, TILES_Y, TILES_Z).astype(jnp.int32)


def steps_of(rng, shape, shards, smallest, high):
    def one(position, shards_of):
        heights = jax.random.uniform(jax.random.fold_in(jax.random.fold_in(rng, 6), position), (shards_of,), jnp.float32, smallest / len(shards), high / len(shards))
        return jnp.repeat(jnp.exp(heights), shape[position] // shards_of).reshape((-1,) + (1,) * (len(shape) - position - 1))

    gain = one(*shards[0])
    for cut in shards[1:]:
        gain = gain * one(*cut)
    return gain


def setup_inputs(seed: int = 0, part: int = 0) -> dict:
    key_of = jax.random.split(jax.random.key(seed), 7)
    part_keys = jax.random.split(jax.random.fold_in(key_of[6], part), 7)
    phase = jnp.clip(0.25 * jax.random.uniform(part_keys[0], (SLOTS, NX, NY, NZ), jnp.float32) ** steps_of(part_keys[0], (SLOTS, NX, NY, NZ), ((1, 4), (2, 2), (3, 2)), -0.2, 0.2), 0.0, 0.25)
    slot_grain = draw_slot_grain(jax.random.fold_in(jax.random.fold_in(key_of[6], part), 71), part)
    crowding = draw_crowding(jax.random.fold_in(jax.random.fold_in(key_of[6], part), 71), part)
    grain_home = jax.random.permutation(part_keys[3], GRAINS).astype(jnp.int32)
    grain_weight = jnp.clip(jnp.exp(jax.random.uniform(part_keys[4], (GRAINS,), jnp.float32, math.log(0.5), math.log(2.0))), 0.5, 2.0)
    grain_target = jnp.clip(jnp.exp(jax.random.uniform(part_keys[5], (GRAINS,), jnp.float32, math.log(0.5), math.log(4.0))), 0.5, 4.0)
    return {"phase": phase, "slot_grain": slot_grain, "crowding": crowding, "grain_home": grain_home, "grain_weight": grain_weight, "grain_target": grain_target}


HIGH = lax.Precision.HIGHEST


def matched(mine, theirs):
    same = (mine[..., :, None] == theirs[..., None, :]) & (mine[..., :, None] >= 0)
    return same.astype(jnp.float32)


def from_side(phase7, slot_ids, axis_k, upward):
    moved = jnp.moveaxis(phase7, (1 + 2 * axis_k, 2 + 2 * axis_k), (1, 2))
    lists = jnp.moveaxis(slot_ids, axis_k, 0)
    empty_list = jnp.full_like(lists[:1], -1)
    if upward:
        edge = moved[:, :, 0]
        other = jnp.concatenate([edge[:, 1:], jnp.zeros_like(edge[:, :1])], axis=1)
        other_lists = jnp.concatenate([lists[1:], empty_list], axis=0)
    else:
        edge = moved[:, :, -1]
        other = jnp.concatenate([jnp.zeros_like(edge[:, :1]), edge[:, :-1]], axis=1)
        other_lists = jnp.concatenate([empty_list, lists[:-1]], axis=0)
    mapping = matched(lists, other_lists)
    remapped = jnp.einsum('tuvab,btupvq->atupvq', mapping, other, precision=HIGH)
    if upward:
        result = jnp.concatenate([moved[:, :, 1:], remapped[:, :, None]], axis=2)
    else:
        result = jnp.concatenate([remapped[:, :, None], moved[:, :, :-1]], axis=2)
    return jnp.moveaxis(result, (1, 2), (1 + 2 * axis_k, 2 + 2 * axis_k))


def spread(table):
    return jnp.transpose(table, (3, 0, 1, 2))[:, :, None, :, None, :, None]


def reference(phase, slot_grain, crowding, grain_home, grain_weight, grain_target):
    live = jnp.arange(SLOTS)[None, None, None, :] < crowding[..., None]
    slot_ids = jnp.where(live, slot_grain, -1)
    safe_ids = jnp.maximum(slot_ids, 0)
    weights = jnp.where(live, grain_weight[safe_ids], jnp.float32(0.0))
    homes = jnp.where(live, grain_home[safe_ids], -1)
    home_hot = (homes[..., None] == jnp.arange(GRAINS)).astype(jnp.float32)
    live7 = spread(live.astype(jnp.float32))
    weight7 = spread(weights)
    phase7 = phase.reshape(SLOTS, TILES_X, CX, TILES_Y, CY, TILES_Z, CZ) * live7
    tile_sums = jnp.sum(phase7, axis=(2, 4, 6))
    volumes = jnp.einsum('stuv,tuvsg->g', tile_sums, home_hot, precision=HIGH)
    multiplier = grain_target - volumes / (CX * CY * CZ)
    drive = spread(jnp.einsum('tuvsg,g->tuvs', home_hot, multiplier, precision=HIGH))
    for section_index in range(STEPS):
        beside_all = jnp.zeros_like(phase7)
        for axis_k in range(3):
            beside_all = beside_all + from_side(phase7, slot_ids, axis_k, True)
            beside_all = beside_all + from_side(phase7, slot_ids, axis_k, False)
        laplace = beside_all - 6.0 * phase7
        weighted = weight7 * phase7 * phase7
        pair = phase7 * weight7 * (jnp.sum(weighted, axis=0, keepdims=True) - weighted)
        update = phase7 + 0.1 * (laplace - 4.0 * pair + 2.0 * drive * phase7 * (1.0 - phase7))
        update = jnp.maximum(update, 0.0)
        total = jnp.sum(update, axis=0, keepdims=True)
        phase7 = update / jnp.maximum(total, 1.0)
    return phase7.reshape(SLOTS, NX, NY, NZ)
```

```python
import functools

import jax
import jax.numpy as jnp
from jax import lax
from jax.experimental import pallas as pl
from jax.experimental.pallas import tpu as pltpu
from jax.sharding import PartitionSpec as P

MESH = pl.DeviceIdType.MESH
CHUNKS = 4
PAD = 8


def each(low, high, body):
    if high - low <= 32:
        for k in range(low, high):
            body(k)
    else:
        pl.loop(low, high)(body)


def kernel(
    sizes, phase, grain, crowd, home, weight, target, out,
    first, second, msg, places, place, coef, xin, yin, zin, zout,
    load_sem, msg_send, msg_recv, place_sem, x_send, x_recv, y_send, y_recv,
    z_send, z_recv, out_sem,
):
    tiles_x, tiles_y, tiles_z = sizes
    slots, cx, cy, cz = phase.shape
    cells = cx * cy * cz
    tiles = tiles_x * tiles_y * tiles_z
    rows = cy // CHUNKS
    tx, ty, tz = (lax.axis_index(a) for a in ("tx", "ty", "tz"))
    me = (tx * tiles_y + ty) * tiles_z + tz
    inner = pl.ds(PAD, cy)

    def partner(k):
        other = lax.rem(me + k, tiles)
        return {
            "tx": lax.div(other, tiles_y * tiles_z),
            "ty": lax.rem(lax.div(other, tiles_z), tiles_y),
            "tz": lax.rem(other, tiles_z),
        }

    loads = [
        pltpu.make_async_copy(phase.at[s], first.at[s, pl.ds(1, cx), inner], load_sem.at[s])
        for s in range(slots)
    ]
    for load in loads:
        load.start()

    barrier = pltpu.get_barrier_semaphore()

    def greet(k):
        pl.semaphore_signal(barrier, inc=1, device_id=partner(k), device_id_type=MESH)

    each(1, tiles, greet)

    for buffer in xin:
        buffer[slots] = jnp.zeros(buffer.shape[1:], jnp.float32)
    for buffer in yin:
        buffer[slots] = jnp.zeros(buffer.shape[1:], jnp.float32)
    for buffer in zin:
        buffer[slots] = jnp.zeros(buffer.shape[1:], jnp.float32)
    live_count = crowd[0, 0, 0]
    row = lax.broadcasted_iota(jnp.int32, (8, cz), 0)
    lane = lax.broadcasted_iota(jnp.int32, (8, cz), 1)
    live = [s < live_count for s in range(slots)]
    ids = [jnp.where(live[s], grain[0, 0, 0, s], -1).astype(jnp.float32) for s in range(slots)]
    mine = [jnp.where(live[s], ids[s], -2.0) for s in range(slots)]
    id_rows = jnp.full((8, cz), -1.0, jnp.float32)
    mine_lanes = jnp.full((8, cz), -2.0, jnp.float32)
    for s in range(slots):
        id_rows = jnp.where(row == s, ids[s], id_rows)
        mine_lanes = jnp.where(lane == s, mine[s], mine_lanes)
    msg[0, 1] = id_rows

    pl.semaphore_wait(barrier, tiles - 1)

    goes = ((tx < tiles_x - 1, ty < tiles_y - 1), (tx > 0, ty > 0))
    comes = ((tx > 0, ty > 0), (tx < tiles_x - 1, ty < tiles_y - 1))
    to = (({"tx": tx + 1}, {"ty": ty + 1}), ({"tx": tx - 1}, {"ty": ty - 1}))

    def x_copy(step, side, c):
        start = c * rows
        if step == 0:
            src = phase.at[:, (cx - 1, 0)[side], pl.ds(start, rows)]
        else:
            src = second.at[:, (cx, 1)[side], pl.ds(PAD + start, rows)]
        at = (step * 2 + side) * CHUNKS + c
        return pltpu.make_async_remote_copy(
            src, xin[at].at[pl.ds(0, slots)], x_send.at[at], x_recv.at[at],
            device_id=to[side][0], device_id_type=MESH,
        )

    def y_copy(step, side):
        at_row = (cy - 1, 0)[side]
        if step == 0:
            src = phase.at[:, :, pl.ds(at_row, 1)]
        else:
            src = second.at[:, pl.ds(1, cx), pl.ds(PAD + at_row, 1)]
        at = step * 2 + side
        return pltpu.make_async_remote_copy(
            src, yin[at].at[pl.ds(0, slots), :, pl.ds(0, 1)], y_send.at[at], y_recv.at[at],
            device_id=to[side][1], device_id_type=MESH,
        )

    def z_copy(step):
        return pltpu.make_async_remote_copy(
            zout[step], zin[step].at[pl.ds(0, slots)], z_send.at[step], z_recv.at[step],
            device_id={"tz": 1 - tz}, device_id_type=MESH,
        )

    def send_x(step, c):
        for side in range(2):
            pl.when(goes[side][0])(lambda: x_copy(step, side, c).start())

    def send_y(step):
        for side in range(2):
            pl.when(goes[side][1])(lambda: y_copy(step, side).start())

    send_y(0)
    send_x(0, 0)

    face_lane = jnp.where(tz == 0, cz - 1, 0)
    lane3 = lax.broadcasted_iota(jnp.int32, (cy, cz), 1)
    z_face = lane3 == face_lane

    def z_part(value, x):
        part = jnp.where(z_face, value, 0.0)
        total = jnp.zeros((8, cz), jnp.float32)
        for t in range(cy // 8):
            total = total + pltpu.roll(part[t * 8:t * 8 + 8], 2 * (x + cx * t), 1)
        return total

    for s in range(slots):
        loads[s].wait()
        factor = jnp.where(live[s], 1.0, 0.0).astype(jnp.float32)

        def clear(x, carry):
            total, face = carry
            value = first[s, x + 1, inner] * factor
            first[s, x + 1, inner] = value
            total = total + jnp.sum(value.reshape(cy // 8, 8, cz), axis=0)
            return total, face + z_part(value, x)

        zero = jnp.zeros((8, cz), jnp.float32)
        total, face = lax.fori_loop(0, cx, clear, (zero, zero))
        zout[0][s] = face
        msg[0, 0, s:s + 1] = jnp.sum(total, axis=0, keepdims=True)

    def msg_copy(k):
        return pltpu.make_async_remote_copy(
            msg.at[0], msg.at[k], msg_send.at[k], msg_recv.at[k],
            device_id=partner(k), device_id_type=MESH,
        )

    each(1, tiles, lambda k: msg_copy(k).start())
    z_copy(0).start()
    for c in range(1, CHUNKS):
        send_x(0, c)
    each(1, tiles, lambda k: msg_copy(k).wait_recv())

    plane = tiles_y * tiles_z
    froms = (
        (plane, comes[0][0]), (tiles - plane, comes[1][0]),
        (tiles_z, comes[0][1]), (tiles - tiles_z, comes[1][1]),
        (tiles - 1, tz == 0), (1, tz == 1),
    )
    table = jnp.zeros((8, cz), jnp.int32)
    for f, (k, there) in enumerate(froms):
        same = (msg[k % tiles, 1] == mine_lanes) & there
        found = jnp.max(jnp.where(same, slots - row, 0), axis=0, keepdims=True)
        table = jnp.where(row == f, slots - found, table)
    places[...] = table
    to_scalars = pltpu.make_async_copy(places, place, place_sem)
    to_scalars.start()

    def add_tile(k, sums):
        ids_k, sums_k = msg[k, 1], msg[k, 0]
        return tuple(
            sums[s] + jnp.where(ids_k == mine[s], sums_k, 0.0) for s in range(slots)
        )

    sums = lax.fori_loop(
        0, tiles, add_tile, (jnp.zeros((8, cz), jnp.float32),) * slots,
        unroll=4 if tiles % 4 == 0 else 1,
    )
    for s in range(slots):
        g = grain[0, 0, 0, s]
        volume = jnp.sum(jnp.sum(sums[s], axis=0, keepdims=True), axis=1, keepdims=True)
        drive = jnp.where(live[s], target[home[g]] - volume * (1.0 / cells), 0.0)
        w = jnp.where(live[s], weight[g], 0.0)
        coef[0, s] = jnp.broadcast_to(0.4 + 0.2 * drive, (8, cz))
        coef[1, s] = jnp.broadcast_to(0.2 * drive, (8, cz))
        coef[2, s] = jnp.full((8, cz), w, jnp.float32)
        coef[3, s] = jnp.full((8, cz), 0.4 * w, jnp.float32)
    to_scalars.wait()

    lane_chunk = lax.broadcasted_iota(jnp.int32, (rows, cz), 1)
    low_lane, high_lane = lane_chunk == 0, lane_chunk == cz - 1

    def advance(step, src, dst, c, x):
        start = PAD + c * rows
        faces = zin[step]
        sub = rows // 8
        wide = lambda i, s: jnp.concatenate([coef[i, s]] * sub, axis=0)
        held, squares, mixed = [], [], jnp.zeros((rows, cz), jnp.float32)
        for s in range(slots):
            p = src[s, x, pl.ds(start, rows)]
            square = wide(2, s) * (p * p)
            mixed = mixed + square
            held.append(p)
            squares.append(square)
        total = jnp.zeros((rows, cz), jnp.float32)
        updates = []
        for s in range(slots):
            p = held[s]
            face = faces[jnp.where(tz == 0, place[4, s], place[5, s])]
            ghost = jnp.concatenate([
                pltpu.roll(face, lax.rem(2 * cz - 2 * ((x - 1) + cx * (c * sub + t)), cz), 1)
                for t in range(sub)
            ], axis=0)
            beside = pltpu.roll(jnp.where(low_lane, ghost, p), cz - 1, 1)
            beside = beside + pltpu.roll(jnp.where(high_lane, ghost, p), 1, 1)
            beside = beside + src[s, x, pl.ds(start - 1, rows)]
            beside = beside + src[s, x, pl.ds(start + 1, rows)]
            beside = beside + src[s, x - 1, pl.ds(start, rows)]
            beside = beside + src[s, x + 1, pl.ds(start, rows)]
            slope = wide(0, s) - wide(1, s) * p - wide(3, s) * (mixed - squares[s])
            update = jnp.maximum(0.1 * beside + p * slope, 0.0)
            total = total + update
            updates.append(update)
        scale = 1.0 / jnp.maximum(total, 1.0)
        for s in range(slots):
            dst[s, x, pl.ds(start, rows)] = updates[s] * scale

    def take_yz(step, src):
        z_copy(step).wait_recv()
        for side in range(2):
            pl.when(comes[side][1])(lambda: y_copy(step, side).wait_recv())
        for side in range(2):
            for s in range(slots):
                ghost_row = (PAD - 1, PAD + cy)[side]
                src[s, pl.ds(1, cx), pl.ds(ghost_row, 1)] = yin[step * 2 + side][
                    place[2 + side, s], :, pl.ds(0, 1)
                ]

    def take_x(step, src, c):
        for side in range(2):
            pl.when(comes[side][0])(lambda: x_copy(step, side, c).wait_recv())
            for s in range(slots):
                src[s, (0, cx + 1)[side], pl.ds(PAD + c * rows, rows)] = xin[
                    (step * 2 + side) * CHUNKS + c
                ][place[side, s]]

    take_yz(0, first)
    for c in range(CHUNKS):
        take_x(0, first, c)
        pl.loop(0, 2)(lambda i: advance(0, first, second, c, 1 + i * (cx - 1)))
        send_x(1, c)
        pl.loop(2, cx)(lambda x: advance(0, first, second, c, x))
    send_y(1)
    for s in range(slots):
        zout[1][s] = lax.fori_loop(
            0, cx, lambda x, face: face + z_part(second[s, x + 1, inner], x),
            jnp.zeros((8, cz), jnp.float32),
        )
    z_copy(1).start()

    def out_copy(i, x, start, count):
        return pltpu.make_async_copy(
            first.at[:, x, pl.ds(PAD + start, count)],
            out.at[:, x - 1, pl.ds(start, count)], out_sem.at[i],
        )

    take_yz(1, second)
    outs = []
    for c in range(CHUNKS):
        pl.loop(2, cx)(lambda x: advance(1, second, first, c, x))
        copy = pltpu.make_async_copy(
            first.at[:, pl.ds(2, cx - 2), pl.ds(PAD + c * rows, rows)],
            out.at[:, pl.ds(1, cx - 2), pl.ds(c * rows, rows)], out_sem.at[c],
        )
        copy.start()
        outs.append(copy)
    for c in range(CHUNKS):
        take_x(1, second, c)
        pl.loop(0, 2)(lambda i: advance(1, second, first, c, 1 + i * (cx - 1)))
        for i, x in enumerate((1, cx)):
            copy = out_copy(CHUNKS * (1 + i) + c, x, c * rows, rows)
            copy.start()
            outs.append(copy)

    each(1, tiles, lambda k: msg_copy(k).wait_send())
    for step in range(2):
        z_copy(step).wait_send()
        for side in range(2):
            pl.when(goes[side][1])(lambda: y_copy(step, side).wait_send())
            for c in range(CHUNKS):
                pl.when(goes[side][0])(lambda: x_copy(step, side, c).wait_send())
    for copy in outs:
        copy.wait()


def on_device(sizes, phase, slot_grain, crowding, grain_home, grain_weight, grain_target):
    slots, cx, cy, cz = phase.shape
    tiles = sizes[0] * sizes[1] * sizes[2]
    field = pltpu.VMEM((slots, cx + 2, cy + 2 * PAD, cz), jnp.float32)
    dma = pltpu.SemaphoreType.DMA
    any_space = pl.BlockSpec(memory_space=pl.ANY)
    scalars = pl.BlockSpec(memory_space=pltpu.SMEM)
    return pl.pallas_call(
        functools.partial(kernel, sizes),
        out_shape=jax.ShapeDtypeStruct(phase.shape, jnp.float32),
        in_specs=[any_space] + [scalars] * 5,
        out_specs=any_space,
        scratch_shapes=[
            field, field,
            pltpu.VMEM((tiles, 2, 8, cz), jnp.float32),
            pltpu.VMEM((8, cz), jnp.int32),
            pltpu.SMEM((8, cz), jnp.int32),
            pltpu.VMEM((4, slots, 8, cz), jnp.float32),
            [pltpu.VMEM((slots + 1, cy // CHUNKS, cz), jnp.float32)] * (4 * CHUNKS),
            [pltpu.VMEM((slots + 1, cx, 8, cz), jnp.float32)] * 4,
            [pltpu.VMEM((slots + 1, 8, cz), jnp.float32)] * 2,
            [pltpu.VMEM((slots, 8, cz), jnp.float32)] * 2,
            dma((slots,)), dma((tiles,)), dma((tiles,)), dma,
            dma((4 * CHUNKS,)), dma((4 * CHUNKS,)), dma((4,)), dma((4,)),
            dma((2,)), dma((2,)), dma((3 * CHUNKS,)),
        ],
        compiler_params=pltpu.CompilerParams(
            collective_id=0, has_side_effects=True, vmem_limit_bytes=40 * 2**20
        ),
    )(phase, slot_grain, crowding, grain_home, grain_weight, grain_target)


def solution(mesh):
    sizes = tuple(mesh.shape[a] for a in ("tx", "ty", "tz"))
    return jax.shard_map(
        functools.partial(on_device, sizes),
        mesh=mesh,
        in_specs=(
            P(None, ("groups", "tx"), "ty", "tz"),
            P(("groups", "tx"), "ty", "tz", None),
            P(("groups", "tx"), "ty", "tz"),
            P("groups"),
            P("groups"),
            P("groups"),
        ),
        out_specs=P(None, ("groups", "tx"), "ty", "tz"),
        check_vma=False,
    )
```

```python
import functools

import jax
import jax.numpy as jnp
from jax import lax
from jax.experimental import pallas as pl
from jax.experimental.pallas import tpu as pltpu
from jax.sharding import PartitionSpec as P

MESH = pl.DeviceIdType.MESH
CHUNKS = 4
PAD = 8


def each(low, high, body):
    if high - low <= 32:
        for k in range(low, high):
            body(k)
    else:
        pl.loop(low, high)(body)


def kernel(
    sizes, phase, grain_in, crowd_in, home_in, weight_in, target_in, out,
    grain, crowd, home, weight, target, first, second, msg, places, place, coef, xin, yin, zin, zout,
    small_sem, load_sem, msg_send, msg_recv, place_sem, x_send, x_recv, y_send, y_recv,
    z_send, z_recv, out_sem,
):
    tiles_x, tiles_y, tiles_z = sizes
    slots, cx, cy, cz = phase.shape
    cells = cx * cy * cz
    tiles = tiles_x * tiles_y * tiles_z
    rows = cy // CHUNKS
    tx, ty, tz = (lax.axis_index(a) for a in ("tx", "ty", "tz"))
    me = (tx * tiles_y + ty) * tiles_z + tz
    inner = pl.ds(PAD, cy)

    def partner(k):
        other = lax.rem(me + k, tiles)
        return {
            "tx": lax.div(other, tiles_y * tiles_z),
            "ty": lax.rem(lax.div(other, tiles_z), tiles_y),
            "tz": lax.rem(other, tiles_z),
        }

    smalls = [
        pltpu.make_async_copy(src, dst, small_sem.at[i])
        for i, (src, dst) in enumerate((
            (crowd_in, crowd), (grain_in, grain), (home_in, home),
            (weight_in, weight), (target_in, target),
        ))
    ]
    for small in smalls:
        small.start()
    loads = [
        pltpu.make_async_copy(phase.at[s], first.at[s, pl.ds(1, cx), inner], load_sem.at[s])
        for s in range(slots)
    ]
    for load in loads:
        load.start()

    barrier = pltpu.get_barrier_semaphore()

    def greet(k):
        pl.semaphore_signal(barrier, inc=1, device_id=partner(k), device_id_type=MESH)

    each(1, tiles, greet)

    for buffer in xin:
        buffer[slots] = jnp.zeros(buffer.shape[1:], jnp.float32)
    for buffer in yin:
        buffer[slots] = jnp.zeros(buffer.shape[1:], jnp.float32)
    for buffer in zin:
        buffer[slots] = jnp.zeros(buffer.shape[1:], jnp.float32)
    for small in smalls:
        small.wait()
    live_count = crowd[0, 0, 0]
    row = lax.broadcasted_iota(jnp.int32, (8, cz), 0)
    lane = lax.broadcasted_iota(jnp.int32, (8, cz), 1)
    live = [s < live_count for s in range(slots)]
    ids = [jnp.where(live[s], grain[0, 0, 0, s], -1).astype(jnp.float32) for s in range(slots)]
    mine = [jnp.where(live[s], ids[s], -2.0) for s in range(slots)]
    id_rows = jnp.full((8, cz), -1.0, jnp.float32)
    mine_lanes = jnp.full((8, cz), -2.0, jnp.float32)
    for s in range(slots):
        id_rows = jnp.where(row == s, ids[s], id_rows)
        mine_lanes = jnp.where(lane == s, mine[s], mine_lanes)
    msg[0, 1] = id_rows

    pl.semaphore_wait(barrier, tiles - 1)

    goes = ((tx < tiles_x - 1, ty < tiles_y - 1), (tx > 0, ty > 0))
    comes = ((tx > 0, ty > 0), (tx < tiles_x - 1, ty < tiles_y - 1))
    to = (({"tx": tx + 1}, {"ty": ty + 1}), ({"tx": tx - 1}, {"ty": ty - 1}))

    def x_copy(step, side, c):
        start = c * rows
        if step == 0:
            src = phase.at[:, (cx - 1, 0)[side], pl.ds(start, rows)]
        else:
            src = second.at[:, (cx, 1)[side], pl.ds(PAD + start, rows)]
        at = (step * 2 + side) * CHUNKS + c
        return pltpu.make_async_remote_copy(
            src, xin[at].at[pl.ds(0, slots)], x_send.at[at], x_recv.at[at],
            device_id=to[side][0], device_id_type=MESH,
        )

    def y_copy(step, side):
        at_row = (cy - 1, 0)[side]
        if step == 0:
            src = phase.at[:, :, pl.ds(at_row, 1)]
        else:
            src = second.at[:, pl.ds(1, cx), pl.ds(PAD + at_row, 1)]
        at = step * 2 + side
        return pltpu.make_async_remote_copy(
            src, yin[at].at[pl.ds(0, slots), :, pl.ds(0, 1)], y_send.at[at], y_recv.at[at],
            device_id=to[side][1], device_id_type=MESH,
        )

    def z_copy(step):
        return pltpu.make_async_remote_copy(
            zout[step], zin[step].at[pl.ds(0, slots)], z_send.at[step], z_recv.at[step],
            device_id={"tz": 1 - tz}, device_id_type=MESH,
        )

    def send_x(step, c):
        for side in range(2):
            pl.when(goes[side][0])(lambda: x_copy(step, side, c).start())

    def send_y(step):
        for side in range(2):
            pl.when(goes[side][1])(lambda: y_copy(step, side).start())

    send_y(0)
    send_x(0, 0)

    for s in range(slots):
        loads[s].wait()
        parts = [jnp.sum(first[s, x + 1, inner].reshape(cy // 8, 8, cz), axis=0) for x in range(cx)]
        while len(parts) > 1:
            parts = [a + b for a, b in zip(parts[::2], parts[1::2])]
        total = jnp.where(live[s], jnp.sum(parts[0], axis=0, keepdims=True), 0.0)
        msg[0, 0, s:s + 1] = total

    def msg_copy(k):
        return pltpu.make_async_remote_copy(
            msg.at[0], msg.at[k], msg_send.at[k], msg_recv.at[k],
            device_id=partner(k), device_id_type=MESH,
        )

    each(1, tiles, lambda k: msg_copy(k).start())

    z_face = lane == jnp.where(tz == 0, cz - 1, 0)

    def pack_z(step, src):
        @pl.loop(0, slots)
        def _(s):
            parts = []
            for x in range(cx):
                for t in range(cy // 8):
                    value = src[s, x + 1, pl.ds(PAD + 8 * t, 8)]
                    part = jnp.where(z_face, value, 0.0)
                    k = x + cx * t
                    parts.append(pltpu.roll(part, 2 * k, 1) if k else part)
            while len(parts) > 1:
                parts = [a + b for a, b in zip(parts[::2], parts[1::2])]
            zout[step][s] = parts[0]

        z_copy(step).start()

    pack_z(0, first)
    for c in range(1, CHUNKS):
        send_x(0, c)
    each(1, tiles, lambda k: msg_copy(k).wait_recv())

    plane = tiles_y * tiles_z
    froms = (
        (plane, comes[0][0]), (tiles - plane, comes[1][0]),
        (tiles_z, comes[0][1]), (tiles - tiles_z, comes[1][1]),
        (tiles - 1, tz == 0), (1, tz == 1),
    )
    table = jnp.zeros((8, cz), jnp.int32)
    for f, (k, there) in enumerate(froms):
        same = (msg[k % tiles, 1] == mine_lanes) & there
        found = jnp.max(jnp.where(same, slots - row, 0), axis=0, keepdims=True)
        table = jnp.where(row == f, slots - found, table)
    places[...] = table
    to_scalars = pltpu.make_async_copy(places, place, place_sem)
    to_scalars.start()

    def add_tile(k, sums):
        ids_k, sums_k = msg[k, 1], msg[k, 0]
        return tuple(
            sums[s] + jnp.where(ids_k == mine[s], sums_k, 0.0) for s in range(slots)
        )

    sums = lax.fori_loop(
        0, tiles, add_tile, (jnp.zeros((8, cz), jnp.float32),) * slots,
        unroll=4 if tiles % 4 == 0 else 1,
    )
    for s in range(slots):
        g = grain[0, 0, 0, s]
        volume = jnp.sum(jnp.sum(sums[s], axis=0, keepdims=True), axis=1, keepdims=True)
        drive = jnp.where(live[s], target[home[g]] - volume * (1.0 / cells), 0.0)
        w = jnp.where(live[s], weight[g], 0.0)
        coef[0, s] = jnp.broadcast_to(jnp.where(live[s], 0.4 + 0.2 * drive, 0.0), (8, cz))
        coef[1, s] = jnp.broadcast_to(0.2 * drive, (8, cz))
        coef[2, s] = jnp.full((8, cz), w, jnp.float32)
        coef[3, s] = jnp.full((8, cz), 0.4 * w, jnp.float32)
        coef[4, s] = jnp.full((8, cz), jnp.where(live[s], 0.1, 0.0), jnp.float32)
    to_scalars.wait()
    z_place = [jnp.where(tz == 0, place[4, s], place[5, s]) for s in range(slots)]

    low_lane, high_lane = lane == 0, lane == cz - 1

    def advance(step, src, dst, c, x):
        for t in range(rows // 8):
            advance_rows(step, src, dst, c * (rows // 8) + t, x)

    def advance_rows(step, src, dst, t, x):
        start = PAD + 8 * t
        faces = zin[step]
        turn = lax.rem(2 * cz - 2 * ((x - 1) + cx * t), cz)
        squares, mixed = [], jnp.zeros((8, cz), jnp.float32)
        for s in range(slots):
            p = src[s, x, pl.ds(start, 8)]
            square = coef[2, s] * (p * p)
            mixed = mixed + square
            squares.append(square)
        total = jnp.zeros((8, cz), jnp.float32)
        updates = []
        for s in range(slots):
            p = src[s, x, pl.ds(start, 8)]
            ghost = pltpu.roll(faces[z_place[s]], turn, 1)
            beside = pltpu.roll(jnp.where(low_lane, ghost, p), cz - 1, 1)
            beside = beside + pltpu.roll(jnp.where(high_lane, ghost, p), 1, 1)
            beside = beside + (src[s, x, pl.ds(start - 1, 8)] + src[s, x, pl.ds(start + 1, 8)])
            beside = beside + (src[s, x - 1, pl.ds(start, 8)] + src[s, x + 1, pl.ds(start, 8)])
            slope = coef[0, s] - coef[1, s] * p - coef[3, s] * (mixed - squares[s])
            update = jnp.maximum(coef[4, s] * beside + p * slope, 0.0)
            total = total + update
            updates.append(update)
        scale = 1.0 / jnp.maximum(total, 1.0)
        for s in range(slots):
            dst[s, x, pl.ds(start, 8)] = updates[s] * scale

    def take_yz(step, src):
        z_copy(step).wait_recv()
        for side in range(2):
            pl.when(comes[side][1])(lambda: y_copy(step, side).wait_recv())
        for side in range(2):
            for s in range(slots):
                ghost_row = (PAD - 1, PAD + cy)[side]
                src[s, pl.ds(1, cx), pl.ds(ghost_row, 1)] = yin[step * 2 + side][
                    place[2 + side, s], :, pl.ds(0, 1)
                ]

    def take_x(step, src, c):
        for side in range(2):
            pl.when(comes[side][0])(lambda: x_copy(step, side, c).wait_recv())
            for s in range(slots):
                src[s, (0, cx + 1)[side], pl.ds(PAD + c * rows, rows)] = xin[
                    (step * 2 + side) * CHUNKS + c
                ][place[side, s]]

    take_yz(0, first)
    for c in range(CHUNKS):
        take_x(0, first, c)
        pl.loop(0, 2)(lambda i: advance(0, first, second, c, 1 + i * (cx - 1)))
        send_x(1, c)
        pl.loop(2, cx)(lambda x: advance(0, first, second, c, x))
    send_y(1)
    pack_z(1, second)

    def out_copy(i, x, start, count):
        return pltpu.make_async_copy(
            first.at[:, x, pl.ds(PAD + start, count)],
            out.at[:, x - 1, pl.ds(start, count)], out_sem.at[i],
        )

    take_yz(1, second)
    outs = []
    for c in range(CHUNKS):
        pl.loop(2, cx)(lambda x: advance(1, second, first, c, x))
        copy = pltpu.make_async_copy(
            first.at[:, pl.ds(2, cx - 2), pl.ds(PAD + c * rows, rows)],
            out.at[:, pl.ds(1, cx - 2), pl.ds(c * rows, rows)], out_sem.at[c],
        )
        copy.start()
        outs.append(copy)
    for c in range(CHUNKS):
        take_x(1, second, c)
        pl.loop(0, 2)(lambda i: advance(1, second, first, c, 1 + i * (cx - 1)))
        for i, x in enumerate((1, cx)):
            copy = out_copy(CHUNKS * (1 + i) + c, x, c * rows, rows)
            copy.start()
            outs.append(copy)

    each(1, tiles, lambda k: msg_copy(k).wait_send())
    for step in range(2):
        z_copy(step).wait_send()
        for side in range(2):
            pl.when(goes[side][1])(lambda: y_copy(step, side).wait_send())
            for c in range(CHUNKS):
                pl.when(goes[side][0])(lambda: x_copy(step, side, c).wait_send())
    for copy in outs:
        copy.wait()


def on_device(sizes, phase, slot_grain, crowding, grain_home, grain_weight, grain_target):
    slots, cx, cy, cz = phase.shape
    tiles = sizes[0] * sizes[1] * sizes[2]
    field = pltpu.VMEM((slots, cx + 2, cy + 2 * PAD, cz), jnp.float32)
    dma = pltpu.SemaphoreType.DMA
    any_space = pl.BlockSpec(memory_space=pl.ANY)
    in_hbm = pl.BlockSpec(memory_space=pltpu.HBM)
    return pl.pallas_call(
        functools.partial(kernel, sizes),
        out_shape=jax.ShapeDtypeStruct(phase.shape, jnp.float32),
        in_specs=[in_hbm] * 6,
        out_specs=any_space,
        scratch_shapes=[
            pltpu.SMEM(slot_grain.shape, jnp.int32), pltpu.SMEM(crowding.shape, jnp.int32),
            pltpu.SMEM(grain_home.shape, jnp.int32), pltpu.SMEM(grain_weight.shape, jnp.float32),
            pltpu.SMEM(grain_target.shape, jnp.float32),
            field, field,
            pltpu.VMEM((tiles, 2, 8, cz), jnp.float32),
            pltpu.VMEM((8, cz), jnp.int32),
            pltpu.SMEM((8, cz), jnp.int32),
            pltpu.VMEM((5, slots, 8, cz), jnp.float32),
            [pltpu.VMEM((slots + 1, cy // CHUNKS, cz), jnp.float32)] * (4 * CHUNKS),
            [pltpu.VMEM((slots + 1, cx, 8, cz), jnp.float32)] * 4,
            [pltpu.VMEM((slots + 1, 8, cz), jnp.float32)] * 2,
            [pltpu.VMEM((slots, 8, cz), jnp.float32)] * 2,
            dma((5,)), dma((slots,)), dma((tiles,)), dma((tiles,)), dma,
            dma((4 * CHUNKS,)), dma((4 * CHUNKS,)), dma((4,)), dma((4,)),
            dma((2,)), dma((2,)), dma((3 * CHUNKS,)),
        ],
        compiler_params=pltpu.CompilerParams(
            collective_id=0, has_side_effects=True, vmem_limit_bytes=62 * 2**20
        ),
    )(phase, slot_grain, crowding, grain_home, grain_weight, grain_target)


def solution(mesh):
    sizes = tuple(mesh.shape[a] for a in ("tx", "ty", "tz"))
    return jax.shard_map(
        functools.partial(on_device, sizes),
        mesh=mesh,
        in_specs=(
            P(None, ("groups", "tx"), "ty", "tz"),
            P(("groups", "tx"), "ty", "tz", None),
            P(("groups", "tx"), "ty", "tz"),
            P("groups"),
            P("groups"),
            P("groups"),
        ),
        out_specs=P(None, ("groups", "tx"), "ty", "tz"),
        check_vma=False,
    )
```

```python
import functools

import jax
import jax.numpy as jnp
from jax import lax
from jax.experimental import pallas as pl
from jax.experimental.pallas import tpu as pltpu
from jax.sharding import PartitionSpec as P

MESH = pl.DeviceIdType.MESH
CHUNKS = 4
PAD = 8


def each(low, high, body):
    if high - low <= 32:
        for k in range(low, high):
            body(k)
    else:
        pl.loop(low, high)(body)


def kernel(
    sizes, phase, grain_in, crowd_in, home_in, weight_in, target_in, out,
    grain, crowd, home, weight, target, first, second, nearby, msg, ids_of, places, place, coef, xin, yin, zin, zout,
    small_sem, load_sem, ids_send, ids_recv, msg_send, msg_recv, place_sem, x_send, x_recv, y_send, y_recv,
    z_send, z_recv, out_sem,
):
    tiles_x, tiles_y, tiles_z = sizes
    slots, cx, cy, cz = phase.shape
    cells = cx * cy * cz
    tiles = tiles_x * tiles_y * tiles_z
    rows = cy // CHUNKS
    tx, ty, tz = (lax.axis_index(a) for a in ("tx", "ty", "tz"))
    me = (tx * tiles_y + ty) * tiles_z + tz
    inner = pl.ds(PAD, cy)

    def partner(k):
        other = lax.rem(me + k, tiles)
        return {
            "tx": lax.div(other, tiles_y * tiles_z),
            "ty": lax.rem(lax.div(other, tiles_z), tiles_y),
            "tz": lax.rem(other, tiles_z),
        }

    smalls = [
        pltpu.make_async_copy(src, dst, small_sem.at[i])
        for i, (src, dst) in enumerate((
            (crowd_in, crowd), (grain_in, grain), (home_in, home),
            (weight_in, weight), (target_in, target),
        ))
    ]
    for small in smalls:
        small.start()
    loads = [
        pltpu.make_async_copy(phase.at[s], first.at[s, pl.ds(1, cx), inner], load_sem.at[s])
        for s in range(slots)
    ]
    for load in loads:
        load.start()

    barrier = pltpu.get_barrier_semaphore()

    def greet(k):
        pl.semaphore_signal(barrier, inc=1, device_id=partner(k), device_id_type=MESH)

    each(1, tiles, greet)

    for buffer in xin:
        buffer[slots] = jnp.zeros(buffer.shape[1:], jnp.float32)
    for buffer in yin:
        buffer[slots] = jnp.zeros(buffer.shape[1:], jnp.float32)
    for buffer in zin:
        buffer[slots] = jnp.zeros(buffer.shape[1:], jnp.float32)
    for small in smalls:
        small.wait()
    live_count = crowd[0, 0, 0]
    row = lax.broadcasted_iota(jnp.int32, (8, cz), 0)
    lane = lax.broadcasted_iota(jnp.int32, (8, cz), 1)
    live = [s < live_count for s in range(slots)]
    ids = [jnp.where(live[s], grain[0, 0, 0, s], -1).astype(jnp.float32) for s in range(slots)]
    mine = [jnp.where(live[s], ids[s], -2.0) for s in range(slots)]
    id_rows = jnp.full((8, cz), -1.0, jnp.float32)
    mine_lanes = jnp.full((8, cz), -2.0, jnp.float32)
    for s in range(slots):
        id_rows = jnp.where(row == s, ids[s], id_rows)
        mine_lanes = jnp.where(lane == s, mine[s], mine_lanes)
    ids_of[0] = id_rows

    pl.semaphore_wait(barrier, tiles - 1)

    goes = ((tx < tiles_x - 1, ty < tiles_y - 1), (tx > 0, ty > 0))
    comes = ((tx > 0, ty > 0), (tx < tiles_x - 1, ty < tiles_y - 1))
    to = (({"tx": tx + 1}, {"ty": ty + 1}), ({"tx": tx - 1}, {"ty": ty - 1}))

    def x_copy(step, side, c):
        start = c * rows
        if step == 0:
            src = phase.at[:, (cx - 1, 0)[side], pl.ds(start, rows)]
        else:
            src = second.at[:, (cx, 1)[side], pl.ds(PAD + start, rows)]
        at = (step * 2 + side) * CHUNKS + c
        return pltpu.make_async_remote_copy(
            src, xin[at].at[pl.ds(0, slots)], x_send.at[at], x_recv.at[at],
            device_id=to[side][0], device_id_type=MESH,
        )

    def y_copy(step, side):
        at_row = (cy - 1, 0)[side]
        if step == 0:
            src = phase.at[:, :, pl.ds(at_row, 1)]
        else:
            src = second.at[:, pl.ds(1, cx), pl.ds(PAD + at_row, 1)]
        at = step * 2 + side
        return pltpu.make_async_remote_copy(
            src, yin[at].at[pl.ds(0, slots), :, pl.ds(0, 1)], y_send.at[at], y_recv.at[at],
            device_id=to[side][1], device_id_type=MESH,
        )

    def z_copy(step):
        return pltpu.make_async_remote_copy(
            zout[step], zin[step].at[pl.ds(0, slots)], z_send.at[step], z_recv.at[step],
            device_id={"tz": 1 - tz}, device_id_type=MESH,
        )

    def send_x(step, c):
        for side in range(2):
            pl.when(goes[side][0])(lambda: x_copy(step, side, c).start())

    def send_y(step):
        for side in range(2):
            pl.when(goes[side][1])(lambda: y_copy(step, side).start())

    def ids_copy(k):
        return pltpu.make_async_remote_copy(
            ids_of.at[0], ids_of.at[k], ids_send.at[k], ids_recv.at[k],
            device_id=partner(k), device_id_type=MESH,
        )

    each(1, tiles, lambda k: ids_copy(k).start())
    send_y(0)
    send_x(0, 0)

    for s in range(slots):
        loads[s].wait()
        parts = [jnp.sum(first[s, x + 1, inner].reshape(cy // 8, 8, cz), axis=0) for x in range(cx)]
        while len(parts) > 1:
            parts = [a + b for a, b in zip(parts[::2], parts[1::2])]
        total = jnp.where(live[s], jnp.sum(parts[0], axis=0, keepdims=True), 0.0)
        msg[0, s:s + 1] = total

    def msg_copy(k):
        return pltpu.make_async_remote_copy(
            msg.at[0], msg.at[k], msg_send.at[k], msg_recv.at[k],
            device_id=partner(k), device_id_type=MESH,
        )

    each(1, tiles, lambda k: msg_copy(k).start())

    z_face = lane == jnp.where(tz == 0, cz - 1, 0)

    def pack_z(step, src):
        @pl.loop(0, slots)
        def _(s):
            parts = []
            for x in range(cx):
                for t in range(cy // 8):
                    value = src[s, x + 1, pl.ds(PAD + 8 * t, 8)]
                    part = jnp.where(z_face, value, 0.0)
                    k = x + cx * t
                    parts.append(pltpu.roll(part, 2 * k, 1) if k else part)
            while len(parts) > 1:
                parts = [a + b for a, b in zip(parts[::2], parts[1::2])]
            zout[step][s] = pltpu.roll(parts[0], 1 - tz, 1)

        z_copy(step).start()

    pack_z(0, first)
    for c in [CHUNKS - 1] + list(range(1, CHUNKS - 1)):
        send_x(0, c)
    each(1, tiles, lambda k: ids_copy(k).wait_recv())

    plane = tiles_y * tiles_z
    froms = (
        (plane, comes[0][0]), (tiles - plane, comes[1][0]),
        (tiles_z, comes[0][1]), (tiles - tiles_z, comes[1][1]),
        (tiles - 1, tz == 0), (1, tz == 1),
    )
    table = jnp.zeros((8, cz), jnp.int32)
    for f, (k, there) in enumerate(froms):
        same = (ids_of[k % tiles] == mine_lanes) & there
        found = jnp.max(jnp.where(same, slots - row, 0), axis=0, keepdims=True)
        table = jnp.where(row == f, slots - found, table)
    places[...] = table
    to_scalars = pltpu.make_async_copy(places, place, place_sem)
    to_scalars.start()

    to_scalars.wait()

    low_lane, high_lane = lane == 0, lane == cz - 1
    from_high = jnp.where(tz == 0, 1.0, 0.0).astype(jnp.float32)
    from_low = 1.0 - from_high

    def tree(parts):
        while len(parts) > 1:
            parts = [a + b for a, b in zip(parts[::2], parts[1::2])] + parts[len(parts) // 2 * 2:]
        return parts[0]

    def take_yz(step, src):
        z_copy(step).wait_recv()
        for side in range(2):
            pl.when(comes[side][1])(lambda: y_copy(step, side).wait_recv())
        for side in range(2):
            for s in range(slots):
                ghost_row = (PAD - 1, PAD + cy)[side]
                src[s, pl.ds(1, cx), pl.ds(ghost_row, 1)] = yin[step * 2 + side][
                    place[2 + side, s], :, pl.ds(0, 1)
                ]

    def sum_nearby(step, src):
        @pl.loop(0, slots)
        def _(s):
            face = zin[step][jnp.where(tz == 0, place[4, s], place[5, s])]
            for x in range(cx):
                for t in range(cy // 8):
                    start = PAD + 8 * t
                    p = src[s, x + 1, pl.ds(start, 8)]
                    k = x + cx * t
                    ghost = jnp.broadcast_to(face[:, 2 * k:2 * k + 1], (8, cz))
                    near = [
                        pltpu.roll(jnp.where(low_lane, ghost * from_high, p), cz - 1, 1),
                        pltpu.roll(jnp.where(high_lane, ghost * from_low, p), 1, 1),
                        src[s, x + 1, pl.ds(start - 1, 8)],
                        src[s, x + 1, pl.ds(start + 1, 8)],
                    ]
                    if x > 0:
                        near.append(src[s, x, pl.ds(start, 8)])
                    if x < cx - 1:
                        near.append(src[s, x + 2, pl.ds(start, 8)])
                    nearby[s, x, pl.ds(8 * t, 8)] = tree(near)

    def advance(step, src, dst, c, x, side=None):
        for t in range(rows // 8):
            start = c * rows + 8 * t
            squares = []
            for s in range(slots):
                p = src[s, x, pl.ds(PAD + start, 8)]
                squares.append(coef[2, s] * (p * p))
            mixed = tree(squares)
            updates = []
            for s in range(slots):
                p = src[s, x, pl.ds(PAD + start, 8)]
                beside = nearby[s, x - 1, pl.ds(start, 8)]
                if side is not None:
                    face = xin[(step * 2 + side) * CHUNKS + c]
                    beside = beside + face[place[side, s], pl.ds(8 * t, 8)]
                slope = coef[0, s] - coef[1, s] * p - coef[3, s] * (mixed - squares[s])
                updates.append(jnp.maximum(coef[4, s] * beside + p * slope, 0.0))
            scale = 1.0 / jnp.maximum(tree(updates), 1.0)
            for s in range(slots):
                dst[s, x, pl.ds(PAD + start, 8)] = updates[s] * scale

    def edges(step, src, dst, c):
        for side in range(2):
            pl.when(comes[side][0])(lambda: x_copy(step, side, c).wait_recv())
        for side in range(2):
            advance(step, src, dst, c, (1, cx)[side], side)

    def inner_layers(step, src, dst, c):
        pl.loop(2, cx)(lambda x: advance(step, src, dst, c, x))

    take_yz(0, first)
    sum_nearby(0, first)
    each(1, tiles, lambda k: msg_copy(k).wait_recv())

    def add_tile(k, sums):
        ids_k, sums_k = ids_of[k], msg[k]
        return tuple(
            sums[s] + jnp.where(ids_k == mine[s], sums_k, 0.0) for s in range(slots)
        )

    sums = lax.fori_loop(
        0, tiles, add_tile, (jnp.zeros((8, cz), jnp.float32),) * slots,
        unroll=4 if tiles % 4 == 0 else 1,
    )
    for s in range(slots):
        g = grain[0, 0, 0, s]
        volume = jnp.sum(jnp.sum(sums[s], axis=0, keepdims=True), axis=1, keepdims=True)
        drive = jnp.where(live[s], target[home[g]] - volume * (1.0 / cells), 0.0)
        w = jnp.where(live[s], weight[g], 0.0)
        coef[0, s] = jnp.broadcast_to(jnp.where(live[s], 0.4 + 0.2 * drive, 0.0), (8, cz))
        coef[1, s] = jnp.broadcast_to(0.2 * drive, (8, cz))
        coef[2, s] = jnp.full((8, cz), w, jnp.float32)
        coef[3, s] = jnp.full((8, cz), 0.4 * w, jnp.float32)
        coef[4, s] = jnp.full((8, cz), jnp.where(live[s], 0.1, 0.0), jnp.float32)
    order = [0, CHUNKS - 1] + list(range(1, CHUNKS - 1))
    for i, c in enumerate(order):
        edges(0, first, second, c)
        send_x(1, c)
        inner_layers(0, first, second, c)
        if i == 1:
            send_y(1)
    pack_z(1, second)

    take_yz(1, second)
    sum_nearby(1, second)
    outs = []

    def put(layers, c):
        low, count = layers
        copy = pltpu.make_async_copy(
            first.at[:, pl.ds(low + 1, count), pl.ds(PAD + c * rows, rows)],
            out.at[:, pl.ds(low, count), pl.ds(c * rows, rows)], out_sem.at[len(outs)],
        )
        copy.start()
        outs.append(copy)

    for c in order:
        inner_layers(1, second, first, c)
        put((1, cx - 2), c)
    for c in order:
        edges(1, second, first, c)
        put((0, 1), c)
        put((cx - 1, 1), c)

    each(1, tiles, lambda k: msg_copy(k).wait_send())
    each(1, tiles, lambda k: ids_copy(k).wait_send())
    for step in range(2):
        z_copy(step).wait_send()
        for side in range(2):
            pl.when(goes[side][1])(lambda: y_copy(step, side).wait_send())
            for c in range(CHUNKS):
                pl.when(goes[side][0])(lambda: x_copy(step, side, c).wait_send())
    for copy in outs:
        copy.wait()


def on_device(sizes, phase, slot_grain, crowding, grain_home, grain_weight, grain_target):
    slots, cx, cy, cz = phase.shape
    tiles = sizes[0] * sizes[1] * sizes[2]
    field = pltpu.VMEM((slots, cx + 2, cy + 2 * PAD, cz), jnp.float32)
    dma = pltpu.SemaphoreType.DMA
    any_space = pl.BlockSpec(memory_space=pl.ANY)
    in_hbm = pl.BlockSpec(memory_space=pltpu.HBM)
    return pl.pallas_call(
        functools.partial(kernel, sizes),
        out_shape=jax.ShapeDtypeStruct(phase.shape, jnp.float32),
        in_specs=[in_hbm] * 6,
        out_specs=any_space,
        scratch_shapes=[
            pltpu.SMEM(slot_grain.shape, jnp.int32), pltpu.SMEM(crowding.shape, jnp.int32),
            pltpu.SMEM(grain_home.shape, jnp.int32), pltpu.SMEM(grain_weight.shape, jnp.float32),
            pltpu.SMEM(grain_target.shape, jnp.float32),
            field, field,
            pltpu.VMEM((slots, cx, cy, cz), jnp.float32),
            pltpu.VMEM((tiles, 8, cz), jnp.float32),
            pltpu.VMEM((tiles, 8, cz), jnp.float32),
            pltpu.VMEM((8, cz), jnp.int32),
            pltpu.SMEM((8, cz), jnp.int32),
            pltpu.VMEM((5, slots, 8, cz), jnp.float32),
            [pltpu.VMEM((slots + 1, cy // CHUNKS, cz), jnp.float32)] * (4 * CHUNKS),
            [pltpu.VMEM((slots + 1, cx, 8, cz), jnp.float32)] * 4,
            [pltpu.VMEM((slots + 1, 8, cz), jnp.float32)] * 2,
            [pltpu.VMEM((slots, 8, cz), jnp.float32)] * 2,
            dma((5,)), dma((slots,)), dma((tiles,)), dma((tiles,)), dma((tiles,)), dma((tiles,)), dma,
            dma((4 * CHUNKS,)), dma((4 * CHUNKS,)), dma((4,)), dma((4,)),
            dma((2,)), dma((2,)), dma((3 * CHUNKS,)),
        ],
        compiler_params=pltpu.CompilerParams(
            collective_id=0, has_side_effects=True, vmem_limit_bytes=62 * 2**20
        ),
    )(phase, slot_grain, crowding, grain_home, grain_weight, grain_target)


def solution(mesh):
    sizes = tuple(mesh.shape[a] for a in ("tx", "ty", "tz"))
    return jax.shard_map(
        functools.partial(on_device, sizes),
        mesh=mesh,
        in_specs=(
            P(None, ("groups", "tx"), "ty", "tz"),
            P(("groups", "tx"), "ty", "tz", None),
            P(("groups", "tx"), "ty", "tz"),
            P("groups"),
            P("groups"),
            P("groups"),
        ),
        out_specs=P(None, ("groups", "tx"), "ty", "tz"),
        check_vma=False,
    )
```
